32 devices in a mesh: ma: 8 (over y, x, core), freq: 4 (over z).
Axes of the slice: x: 2, y: 2, z: 4, core: 2. Of those that a mesh axis runs over, the one named last changes fastest.
Arguments:
- visibilities: bfloat16 [2, 4096, 8, 1024], P(None, 'ma', 'freq'), may hold values from -0.099609375 to 0.099609375
- beam_modes: bfloat16 [32, 8, 2, 32, 1024], P('ma', 'freq'), may hold values from -0.125 to 0.125
- kl_vectors: bfloat16 [32, 2, 256, 256], P('ma', None, None, 'freq'), may hold values from -0.25 to 0.25
Outputs:
- kl_coeffs: float32 [32, 2, 256], P('ma', None, 'freq')
The draws below stay inside these ranges and needn't reach their ends.
All inputs are finite; a program needn't handle non-finite values.
Results may differ from the reference program's by a relative error of at most 0.0046.
Values may be sent and summed in bfloat16 or wider, within the bound.
A program may use at most 64 MiB of HBM per device.

```python
import math
import jax
import jax.numpy as jnp
from jax import lax

NT = 4096
B = 1024
S = 32
KL = 256
M = 32
F = 8


def shard_levels(key, dims, cuts, least, high):
    gain = 1.0
    for position, shards_of in cuts:
        steps = jax.random.uniform(jax.random.fold_in(jax.random.fold_in(key, 6), position), (shards_of,), jnp.float32, least / len(cuts), high / len(cuts))
        gain = gain * jnp.repeat(jnp.exp(steps), dims[position] // shards_of).reshape((-1,) + (1,) * (len(dims) - 1 - position))
    return gain


def bell_draw(stream_key, dims, scale, reach, cuts=(), kind=jnp.bfloat16):
    values = scale * jax.random.normal(stream_key, dims, jnp.float32)
    if cuts:
        values = values * shard_levels(stream_key, dims, cuts, -0.22, 0.18)
    return jnp.clip(values, -reach, reach).astype(kind)


def setup_inputs(seed: int = 0) -> dict:
    keys = jax.random.split(jax.random.key(seed), 4)
    visibilities = bell_draw(keys[0], (2, NT, F, B), 0.015625, 0.099609375, ((1, 8), (2, 4)))
    beam_modes = bell_draw(keys[1], (M, F, 2, S, B), (2 * B) ** -0.5, 0.125, ((0, 8), (1, 4)))
    kl_vectors = bell_draw(keys[2], (M, 2, KL, F * S), (2 * F * S) ** -0.5, 0.25, ((0, 8), (3, 4)))
    return {"visibilities": visibilities, "beam_modes": beam_modes, "kl_vectors": kl_vectors}


def phase_table(mode_total):
    mode_ids = jnp.arange(mode_total, dtype=jnp.int32)
    time_ids = jnp.arange(NT, dtype=jnp.int32)
    phase_turns = (mode_ids[:, None] * time_ids[None, :]) % NT
    radians = phase_turns.astype(jnp.float32) * (2.0 * math.pi / NT)
    cosine = jnp.cos(radians)
    sine = jnp.sin(radians)
    twiddle = jnp.stack([jnp.stack([cosine, sine], 1), jnp.stack([-sine, cosine], 1)], 1)
    return twiddle.astype(jnp.bfloat16)


def reference(visibilities, beam_modes, kl_vectors):
    twiddle = phase_table(M).reshape(2 * M, 2 * NT)
    flat_rows = visibilities.reshape(2 * NT, F * B)
    spectra = jnp.dot(twiddle, flat_rows, preferred_element_type=jnp.float32)
    spectra = spectra.astype(jnp.bfloat16).reshape(M, 2, F, B)

    def per_mode(mode_inputs):
        spectrum, beam_rows, kl_rows = mode_inputs
        products = jnp.einsum("fwsb,cfb->wcfs", beam_rows.astype(jnp.float32), spectrum.astype(jnp.float32))
        real_part = products[0, 0] - products[1, 1]
        imag_part = products[1, 0] + products[0, 1]
        projected = jnp.stack([real_part, imag_part]).astype(jnp.bfloat16).reshape(2, F * S)
        coupled = jnp.einsum("wkx,cx->wck", kl_rows.astype(jnp.float32), projected.astype(jnp.float32))
        return jnp.stack([coupled[0, 0] - coupled[1, 1], coupled[0, 1] + coupled[1, 0]])

    return lax.map(per_mode, (spectra, beam_modes, kl_vectors))
```

```python
import functools
import math

import jax
import jax.numpy as jnp
import numpy as np
from jax import lax
from jax.experimental import pallas as pl
from jax.experimental.pallas import tpu as pltpu
from jax.sharding import PartitionSpec as P

NT = 4096
LANES = 128
GROUP = 2
MESH = pl.DeviceIdType.MESH


def steps(count, body):
    if count <= 16:
        for i in range(count):
            body(i)
    else:
        lax.fori_loop(0, count, lambda i, c: (body(i), c)[1], 0)


def twiddle_rows(xp, first, time_count, modes, owners, fcount):
    m = xp.arange(owners * modes, dtype=xp.int32)
    t = first + xp.arange(time_count, dtype=xp.int32)
    turns = (m[:, None] * t[None, :]) % NT
    angle = turns.astype(xp.float32) * xp.float32(2.0 * math.pi / NT)
    cos, sin = xp.cos(angle), xp.sin(angle)
    table = xp.stack([xp.stack([cos, sin], 1), xp.stack([-sin, cos], 1)], 1)
    table = table.reshape(owners, modes, 2, 2, time_count).transpose(0, 2, 1, 3, 4)
    eye = xp.eye(fcount, dtype=xp.float32)
    full = table[:, :, :, None, :, :, None] * eye[:, None, None, :]
    return full.reshape(owners * 2 * modes * fcount, 2 * time_count * fcount)


def kernel(
    cfg, vis, table, beam, kl, out,
    vbuf, tw, bbuf, kbuf, total, send, recv, stage, zrecv,
    in_sem, ssem, rsem, zs_sem, zr_sem,
):
    n, nf, modes, fcount, kd, ntiles, table_whole = cfg
    groups = ntiles // GROUP
    wide = GROUP * LANES
    rows = 2 * modes * fcount
    half = modes * fcount
    me = lax.axis_index("ma")
    mine = lax.axis_index("freq")

    tw_copy = pltpu.make_async_copy(table.at[me] if table_whole else table, tw, in_sem.at[ntiles])
    tw_copy.start()
    vis_copies = []
    for b in range(ntiles):
        copy = pltpu.make_async_copy(
            vis.at[:, :, b * LANES:(b + 1) * LANES], vbuf.at[b], in_sem.at[b])
        copy.start()
        vis_copies.append(copy)
    late = []
    for w in range(2):
        late.append(pltpu.make_async_copy(beam.at[:, :, w], bbuf.at[w], in_sem.at[ntiles + 1 + w]))
        late.append(pltpu.make_async_copy(kl.at[:, w], kbuf.at[w], in_sem.at[ntiles + 3 + w]))
    for copy in late:
        copy.start()

    barrier = pltpu.get_barrier_semaphore()

    def greet_ma(o):
        pl.semaphore_signal(barrier, inc=1, device_id=(lax.rem(me + o + 1, n), mine), device_id_type=MESH)

    def greet_freq(o):
        pl.semaphore_signal(barrier, inc=1, device_id=(me, lax.rem(mine + o + 1, nf)), device_id_type=MESH)

    steps(n - 1, greet_ma)
    steps(nf - 1, greet_freq)

    def block_copy(g, o):
        peer = lax.rem(me + o + 1, n)
        return pltpu.make_async_remote_copy(
            src_ref=send.at[g, peer], dst_ref=recv.at[g, o],
            send_sem=ssem.at[g, o], recv_sem=rsem.at[g, o],
            device_id=(peer, mine), device_id_type=MESH)

    tw_copy.wait()
    for g in range(groups):
        pieces = []
        for b in range(g * GROUP, (g + 1) * GROUP):
            vis_copies[b].wait()
            pieces.append(vbuf.at[b].reshape(vbuf.shape[1] * fcount, LANES)[...])
        part = jnp.dot(tw[...], jnp.concatenate(pieces, 1), preferred_element_type=jnp.float32)
        total[g] = part.reshape(n, rows, wide)
        send[g] = part.reshape(n, rows, wide).astype(jnp.bfloat16)
        if g == 0:
            pl.semaphore_wait(barrier, n + nf - 2)
        steps(n - 1, lambda o: block_copy(g, o).start())

    for copy in late:
        copy.wait()
    acc = jnp.zeros((rows, half * bbuf.shape[3]), jnp.float32)
    for g in range(groups):
        steps(n - 1, lambda o: block_copy(g, o).wait_recv())
        spec = total[g, me]
        if n <= 16:
            for o in range(n - 1):
                spec = spec + recv[g, o].astype(jnp.float32)
        else:
            spec = lax.fori_loop(0, n - 1, lambda o, s: s + recv[g, o].astype(jnp.float32), spec)
        turned = jnp.concatenate([-spec[half:], spec[:half]], 0)
        for w, lhs in ((0, spec), (1, turned)):
            rhs = bbuf[w, :, :, :, g * wide:(g + 1) * wide].reshape(-1, wide)
            acc = acc + lax.dot_general(
                lhs.astype(jnp.bfloat16), rhs, (((1,), (1,)), ((), ())),
                preferred_element_type=jnp.float32)

    svd = bbuf.shape[3]
    cols = half * svd
    row = lax.broadcasted_iota(jnp.int32, (half, cols), 0)
    lane = lax.broadcasted_iota(jnp.int32, (half, cols), 1)
    own = row == lane // svd
    real = jnp.sum(jnp.where(own, acc[:half], 0.0), 0, keepdims=True)
    imag = jnp.sum(jnp.where(own, acc[half:], 0.0), 0, keepdims=True)
    row = lax.broadcasted_iota(jnp.int32, (2 * modes, cols), 0)
    lane = lax.broadcasted_iota(jnp.int32, (2 * modes, cols), 1)
    own = row // 2 == lane // (fcount * svd)
    first = row % 2 == 0
    straight = jnp.where(own, jnp.where(first, real, imag), 0.0).astype(jnp.bfloat16)
    crossed = jnp.where(own, jnp.where(first, -imag, real), 0.0).astype(jnp.bfloat16)
    coeffs = jnp.dot(straight, kbuf[0].reshape(cols, -1), preferred_element_type=jnp.float32)
    coeffs = coeffs + jnp.dot(crossed, kbuf[1].reshape(cols, -1), preferred_element_type=jnp.float32)
    for i in range(stage.shape[0]):
        stage[i] = coeffs[:, i * LANES:(i + 1) * LANES]

    share = LANES // kd

    def kl_copy(o):
        peer = lax.rem(mine + o + 1, nf)
        return pltpu.make_async_remote_copy(
            src_ref=stage.at[peer // share], dst_ref=zrecv.at[o],
            send_sem=zs_sem.at[o], recv_sem=zr_sem.at[o],
            device_id=(me, peer), device_id_type=MESH)

    steps(nf - 1, lambda o: kl_copy(o).start())
    mixed = stage[mine // share]
    steps(nf - 1, lambda o: kl_copy(o).wait_recv())
    for o in range(nf - 1):
        mixed = mixed + zrecv[o]
    result = mixed[:, :kd]
    for i in range(1, share):
        result = jnp.where(mine % share == i, mixed[:, i * kd:(i + 1) * kd], result)
    for m in range(modes):
        out[m] = result[2 * m:2 * m + 2]
    for g in range(groups):
        steps(n - 1, lambda o: block_copy(g, o).wait_send())
    steps(nf - 1, lambda o: kl_copy(o).wait_send())


def shards(visibilities, beam_modes, kl_vectors):
    n, nf = lax.axis_size("ma"), lax.axis_size("freq")
    parts, times, fcount, bases = visibilities.shape
    modes, _, _, svd, _ = beam_modes.shape
    klen, xs = kl_vectors.shape[2:]
    kd = klen // nf
    ntiles = bases // LANES
    groups, wide = ntiles // GROUP, GROUP * LANES
    rows = 2 * modes * fcount
    table_rows, table_cols = n * rows, parts * times * fcount
    table_whole = n * table_rows * table_cols <= 1 << 22
    if table_whole:
        table = jnp.asarray(np.stack([
            twiddle_rows(np, a * times, times, modes, n, fcount) for a in range(n)
        ]).astype(jnp.bfloat16))
    else:
        first = lax.axis_index("ma") * times
        table = twiddle_rows(jnp, first, times, modes, n, fcount).astype(jnp.bfloat16)
    cfg = (n, nf, modes, fcount, kd, ntiles, table_whole)
    f32, bf16 = jnp.float32, jnp.bfloat16
    dma = pltpu.SemaphoreType.DMA
    return pl.pallas_call(
        functools.partial(kernel, cfg),
        out_shape=jax.ShapeDtypeStruct((modes, 2, kd), f32),
        in_specs=[pl.BlockSpec(memory_space=pl.ANY)] * 4,
        out_specs=pl.BlockSpec(memory_space=pltpu.VMEM),
        scratch_shapes=[
            pltpu.VMEM((ntiles, parts * times, fcount, LANES), bf16),
            pltpu.VMEM((table_rows, table_cols), bf16),
            pltpu.VMEM((2, modes, fcount, svd, bases), bf16),
            pltpu.VMEM((2, modes, xs, klen), bf16),
            pltpu.VMEM((groups, n, rows, wide), f32),
            pltpu.VMEM((groups, n, rows, wide), bf16),
            pltpu.VMEM((groups, n - 1, rows, wide), bf16),
            pltpu.VMEM((klen // LANES, 2 * modes, LANES), f32),
            pltpu.VMEM((nf - 1, 2 * modes, LANES), f32),
            dma((ntiles + 5,)),
            dma((groups, n - 1)),
            dma((groups, n - 1)),
            dma((nf - 1,)),
            dma((nf - 1,)),
        ],
        compiler_params=pltpu.CompilerParams(
            collective_id=0, has_side_effects=True, vmem_limit_bytes=40 << 20),
    )(
        visibilities.reshape(parts * times, fcount, bases),
        table,
        beam_modes,
        kl_vectors.transpose(0, 1, 3, 2),
    )


def solution(mesh):
    in_specs = (
        P(None, "ma", "freq", None),
        P("ma", "freq", None, None, None),
        P("ma", None, None, "freq"),
    )
    out_specs = P("ma", None, "freq")
    return jax.shard_map(shards, mesh=mesh, in_specs=in_specs, out_specs=out_specs, check_vma=False)
```

```python
import functools
import math

import jax
import jax.numpy as jnp
import numpy as np
from jax import lax
from jax.experimental import pallas as pl
from jax.experimental.pallas import tpu as pltpu
from jax.sharding import PartitionSpec as P

NT = 4096
LANES = 128
GROUP = 2
MESH = pl.DeviceIdType.MESH


def steps(count, body):
    if count <= 16:
        for i in range(count):
            body(i)
    else:
        lax.fori_loop(0, count, lambda i, c: (body(i), c)[1], 0)


def twiddle_rows(xp, first, time_count, modes, owners, fcount):
    m = xp.arange(owners * modes, dtype=xp.int32)
    t = first + xp.arange(time_count, dtype=xp.int32)
    turns = (m[:, None] * t[None, :]) % NT
    angle = turns.astype(xp.float32) * xp.float32(2.0 * math.pi / NT)
    cos, sin = xp.cos(angle), xp.sin(angle)
    table = xp.stack([xp.stack([cos, sin], 1), xp.stack([-sin, cos], 1)], 1)
    table = table.reshape(owners, modes, 2, 2, time_count).transpose(0, 2, 1, 3, 4)
    eye = xp.eye(fcount, dtype=xp.float32)
    full = table[:, :, :, None, :, :, None] * eye[:, None, None, :]
    return full.reshape(owners * 2 * modes * fcount, 2 * time_count * fcount)


def kernel(
    cfg, vis, table, beam, kl, out,
    vbuf, tw, bbuf, kbuf, total, send, recv, stage, zrecv,
    in_sem, ssem, rsem, zs_sem, zr_sem,
):
    n, nf, modes, fcount, kd, ntiles, table_whole = cfg
    groups = ntiles // GROUP
    wide = GROUP * LANES
    rows = 2 * modes * fcount
    half = modes * fcount
    me = lax.axis_index("ma")
    mine = lax.axis_index("freq")

    tw_copy = pltpu.make_async_copy(table.at[me] if table_whole else table, tw, in_sem.at[ntiles])
    tw_copy.start()
    vis_copies = []
    for b in range(ntiles):
        copy = pltpu.make_async_copy(
            vis.at[:, :, b * LANES:(b + 1) * LANES], vbuf.at[b], in_sem.at[b])
        copy.start()
        vis_copies.append(copy)
    late = []
    for w in range(2):
        late.append(pltpu.make_async_copy(beam.at[:, :, w], bbuf.at[w], in_sem.at[ntiles + 1 + w]))
        late.append(pltpu.make_async_copy(kl.at[:, w], kbuf.at[w], in_sem.at[ntiles + 3 + w]))
    for copy in late:
        copy.start()

    barrier = pltpu.get_barrier_semaphore()

    def greet_ma(o):
        pl.semaphore_signal(barrier, inc=1, device_id=(lax.rem(me + o + 1, n), mine), device_id_type=MESH)

    def greet_freq(o):
        pl.semaphore_signal(barrier, inc=1, device_id=(me, lax.rem(mine + o + 1, nf)), device_id_type=MESH)

    steps(n - 1, greet_ma)
    steps(nf - 1, greet_freq)

    def block_copy(g, o):
        peer = lax.rem(me + o + 1, n)
        return pltpu.make_async_remote_copy(
            src_ref=send.at[g, peer], dst_ref=recv.at[g, o],
            send_sem=ssem.at[g, o], recv_sem=rsem.at[g, o],
            device_id=(peer, mine), device_id_type=MESH)

    tw_copy.wait()
    for g in range(groups):
        pieces = []
        for b in range(g * GROUP, (g + 1) * GROUP):
            vis_copies[b].wait()
            pieces.append(vbuf.at[b].reshape(vbuf.shape[1] * fcount, LANES)[...])
        part = jnp.dot(tw[...], jnp.concatenate(pieces, 1), preferred_element_type=jnp.float32)
        total[g] = part.reshape(n, rows, wide)
        send[g] = part.reshape(n, rows, wide).astype(jnp.bfloat16)
        if g == 0:
            pl.semaphore_wait(barrier, n + nf - 2)
        steps(n - 1, lambda o: block_copy(g, o).start())

    for copy in late:
        copy.wait()
    acc = jnp.zeros((rows, half * bbuf.shape[3]), jnp.float32)
    for g in range(groups):
        steps(n - 1, lambda o: block_copy(g, o).wait_recv())
        spec = total[g, me]
        if n <= 16:
            for o in range(n - 1):
                spec = spec + recv[g, o].astype(jnp.float32)
        else:
            spec = lax.fori_loop(0, n - 1, lambda o, s: s + recv[g, o].astype(jnp.float32), spec)
        turned = jnp.concatenate([-spec[half:], spec[:half]], 0)
        for w, lhs in ((0, spec), (1, turned)):
            rhs = bbuf[w, :, :, :, g * wide:(g + 1) * wide].reshape(-1, wide)
            acc = acc + lax.dot_general(
                lhs.astype(jnp.bfloat16), rhs, (((1,), (1,)), ((), ())),
                preferred_element_type=jnp.float32)

    svd = bbuf.shape[3]
    cols = half * svd
    row = lax.broadcasted_iota(jnp.int32, (half, cols), 0)
    lane = lax.broadcasted_iota(jnp.int32, (half, cols), 1)
    own = row == lane // svd
    real = jnp.sum(jnp.where(own, acc[:half], 0.0), 0, keepdims=True)
    imag = jnp.sum(jnp.where(own, acc[half:], 0.0), 0, keepdims=True)
    row = lax.broadcasted_iota(jnp.int32, (2 * modes, cols), 0)
    lane = lax.broadcasted_iota(jnp.int32, (2 * modes, cols), 1)
    own = row // 2 == lane // (fcount * svd)
    first = row % 2 == 0
    straight = jnp.where(own, jnp.where(first, real, imag), 0.0).astype(jnp.bfloat16)
    crossed = jnp.where(own, jnp.where(first, -imag, real), 0.0).astype(jnp.bfloat16)
    coeffs = jnp.dot(straight, kbuf[0].reshape(cols, -1), preferred_element_type=jnp.float32)
    coeffs = coeffs + jnp.dot(crossed, kbuf[1].reshape(cols, -1), preferred_element_type=jnp.float32)
    for i in range(stage.shape[0]):
        stage[i] = coeffs[:, i * LANES:(i + 1) * LANES]

    share = LANES // kd

    def kl_copy(o):
        peer = lax.rem(mine + o + 1, nf)
        return pltpu.make_async_remote_copy(
            src_ref=stage.at[peer // share], dst_ref=zrecv.at[o],
            send_sem=zs_sem.at[o], recv_sem=zr_sem.at[o],
            device_id=(me, peer), device_id_type=MESH)

    steps(nf - 1, lambda o: kl_copy(o).start())
    mixed = stage[mine // share]
    steps(nf - 1, lambda o: kl_copy(o).wait_recv())
    for o in range(nf - 1):
        mixed = mixed + zrecv[o]
    result = mixed[:, :kd]
    for i in range(1, share):
        result = jnp.where(mine % share == i, mixed[:, i * kd:(i + 1) * kd], result)
    for m in range(modes):
        out[m] = result[2 * m:2 * m + 2]
    for g in range(groups):
        steps(n - 1, lambda o: block_copy(g, o).wait_send())
    steps(nf - 1, lambda o: kl_copy(o).wait_send())


def shards(visibilities, beam_modes, kl_vectors):
    n, nf = lax.axis_size("ma"), lax.axis_size("freq")
    parts, times, fcount, bases = visibilities.shape
    modes, _, _, svd, _ = beam_modes.shape
    klen, xs = kl_vectors.shape[2:]
    kd = klen // nf
    ntiles = bases // LANES
    groups, wide = ntiles // GROUP, GROUP * LANES
    rows = 2 * modes * fcount
    table_rows, table_cols = n * rows, parts * times * fcount
    table_whole = n * table_rows * table_cols <= 1 << 22
    if table_whole:
        table = jnp.asarray(np.stack([
            twiddle_rows(np, a * times, times, modes, n, fcount) for a in range(n)
        ]).astype(jnp.bfloat16))
    else:
        first = lax.axis_index("ma") * times
        table = twiddle_rows(jnp, first, times, modes, n, fcount).astype(jnp.bfloat16)
    cfg = (n, nf, modes, fcount, kd, ntiles, table_whole)
    f32, bf16 = jnp.float32, jnp.bfloat16
    dma = pltpu.SemaphoreType.DMA
    return pl.pallas_call(
        functools.partial(kernel, cfg),
        out_shape=jax.ShapeDtypeStruct((modes, 2, kd), f32),
        in_specs=[pl.BlockSpec(memory_space=pl.ANY)] * 4,
        out_specs=pl.BlockSpec(memory_space=pltpu.VMEM),
        scratch_shapes=[
            pltpu.VMEM((ntiles, parts * times, fcount, LANES), bf16),
            pltpu.VMEM((table_rows, table_cols), bf16),
            pltpu.VMEM((2, modes, fcount, svd, bases), bf16),
            pltpu.VMEM((2, modes, xs, klen), bf16),
            pltpu.VMEM((groups, n, rows, wide), f32),
            pltpu.VMEM((groups, n, rows, wide), bf16),
            pltpu.VMEM((groups, n - 1, rows, wide), bf16),
            pltpu.VMEM((klen // LANES, 2 * modes, LANES), f32),
            pltpu.VMEM((nf - 1, 2 * modes, LANES), f32),
            dma((ntiles + 5,)),
            dma((groups, n - 1)),
            dma((groups, n - 1)),
            dma((nf - 1,)),
            dma((nf - 1,)),
        ],
        compiler_params=pltpu.CompilerParams(
            collective_id=0, has_side_effects=True, vmem_limit_bytes=60 << 20),
    )(
        visibilities.reshape(parts * times, fcount, bases),
        table,
        beam_modes,
        kl_vectors.transpose(0, 1, 3, 2),
    )


def solution(mesh):
    in_specs = (
        P(None, "ma", "freq", None),
        P("ma", "freq", None, None, None),
        P("ma", None, None, "freq"),
    )
    out_specs = P("ma", None, "freq")
    return jax.shard_map(shards, mesh=mesh, in_specs=in_specs, out_specs=out_specs, check_vma=False)
```

```python
import functools
import math

import jax
import jax.numpy as jnp
import numpy as np
from jax import lax
from jax.experimental import pallas as pl
from jax.experimental.pallas import tpu as pltpu
from jax.sharding import PartitionSpec as P

NT = 4096
LANES = 128
GROUP = 2
MESH = pl.DeviceIdType.MESH


def steps(count, body):
    if count <= 16:
        for i in range(count):
            body(i)
    else:
        lax.fori_loop(0, count, lambda i, c: (body(i), c)[1], 0)


def twiddle_rows(xp, first, time_count, modes, owners, fcount):
    m = xp.arange(owners * modes, dtype=xp.int32)
    t = first + xp.arange(time_count, dtype=xp.int32)
    turns = (m[:, None] * t[None, :]) % NT
    angle = turns.astype(xp.float32) * xp.float32(2.0 * math.pi / NT)
    cos, sin = xp.cos(angle), xp.sin(angle)
    table = xp.stack([xp.stack([cos, sin], 1), xp.stack([-sin, cos], 1)], 1)
    table = table.reshape(owners, modes, 2, 2, time_count).transpose(0, 2, 1, 3, 4)
    eye = xp.eye(fcount, dtype=xp.float32)
    full = table[:, :, :, None, :, :, None] * eye[:, None, None, :]
    return full.reshape(owners * 2 * modes * fcount, 2 * time_count * fcount)


def kernel(
    cfg, vis, table, beam, kl, out,
    vbuf, tw, bbuf, kbuf, total, send, recv, stage, zrecv,
    in_sem, ssem, rsem, zs_sem, zr_sem,
):
    n, nf, modes, fcount, kd, ntiles, table_whole = cfg
    groups = ntiles // GROUP
    wide = GROUP * LANES
    rows = 2 * modes * fcount
    half = modes * fcount
    me = lax.axis_index("ma")
    mine = lax.axis_index("freq")

    tw_copy = pltpu.make_async_copy(table.at[me] if table_whole else table, tw, in_sem.at[ntiles])
    tw_copy.start()
    vis_copies = []
    for b in range(ntiles):
        copy = pltpu.make_async_copy(
            vis.at[:, :, b * LANES:(b + 1) * LANES], vbuf.at[b], in_sem.at[b])
        copy.start()
        vis_copies.append(copy)
    late = []
    for w in range(2):
        late.append(pltpu.make_async_copy(beam.at[:, :, w], bbuf.at[w], in_sem.at[ntiles + 1 + w]))
        late.append(pltpu.make_async_copy(kl.at[:, w], kbuf.at[w], in_sem.at[ntiles + 3 + w]))
    for copy in late:
        copy.start()

    barrier = pltpu.get_barrier_semaphore()

    def greet_ma(o):
        pl.semaphore_signal(barrier, inc=1, device_id=(lax.rem(me + o + 1, n), mine), device_id_type=MESH)

    def greet_freq(o):
        pl.semaphore_signal(barrier, inc=1, device_id=(me, lax.rem(mine + o + 1, nf)), device_id_type=MESH)

    steps(n - 1, greet_ma)
    steps(nf - 1, greet_freq)

    def block_copy(g, o):
        peer = lax.rem(me + o + 1, n)
        return pltpu.make_async_remote_copy(
            src_ref=send.at[g, peer], dst_ref=recv.at[g, o],
            send_sem=ssem.at[g, o], recv_sem=rsem.at[g, o],
            device_id=(peer, mine), device_id_type=MESH)

    tw_copy.wait()
    for g in range(groups):
        pieces = []
        for b in range(g * GROUP, (g + 1) * GROUP):
            vis_copies[b].wait()
            pieces.append(vbuf.at[b].reshape(vbuf.shape[1] * fcount, LANES)[...])
        part = jnp.dot(tw[...], jnp.concatenate(pieces, 1), preferred_element_type=jnp.float32)
        total[g] = part.reshape(n, rows, wide)
        send[g] = part.reshape(n, rows, wide).astype(jnp.bfloat16)
        if g == 0:
            pl.semaphore_wait(barrier, n + nf - 2)
        steps(n - 1, lambda o: block_copy(g, o).start())

    for copy in late:
        copy.wait()
    acc = jnp.zeros((rows, half * bbuf.shape[3]), jnp.float32)
    for g in range(groups):
        steps(n - 1, lambda o: block_copy(g, o).wait_recv())
        spec = total[g, me]
        if n <= 16:
            for o in range(n - 1):
                spec = spec + recv[g, o].astype(jnp.float32)
        else:
            spec = lax.fori_loop(0, n - 1, lambda o, s: s + recv[g, o].astype(jnp.float32), spec)
        turned = jnp.concatenate([-spec[half:], spec[:half]], 0)
        for w, lhs in ((0, spec), (1, turned)):
            rhs = bbuf[w, :, :, :, g * wide:(g + 1) * wide].reshape(-1, wide)
            acc = acc + lax.dot_general(
                lhs.astype(jnp.bfloat16), rhs, (((1,), (1,)), ((), ())),
                preferred_element_type=jnp.float32)

    svd = bbuf.shape[3]
    cols = half * svd
    row = lax.broadcasted_iota(jnp.int32, (half, cols), 0)
    lane = lax.broadcasted_iota(jnp.int32, (half, cols), 1)
    own = row == lane // svd
    real = jnp.sum(jnp.where(own, acc[:half], 0.0), 0, keepdims=True)
    imag = jnp.sum(jnp.where(own, acc[half:], 0.0), 0, keepdims=True)
    row = lax.broadcasted_iota(jnp.int32, (2 * modes, cols), 0)
    lane = lax.broadcasted_iota(jnp.int32, (2 * modes, cols), 1)
    own = row // 2 == lane // (fcount * svd)
    first = row % 2 == 0
    straight = jnp.where(own, jnp.where(first, real, imag), 0.0).astype(jnp.bfloat16)
    crossed = jnp.where(own, jnp.where(first, -imag, real), 0.0).astype(jnp.bfloat16)
    coeffs = jnp.dot(straight, kbuf[0].reshape(cols, -1), preferred_element_type=jnp.float32)
    coeffs = coeffs + jnp.dot(crossed, kbuf[1].reshape(cols, -1), preferred_element_type=jnp.float32)
    for i in range(stage.shape[0]):
        stage[i] = coeffs[:, i * LANES:(i + 1) * LANES]

    share = LANES // kd

    def kl_copy(o):
        peer = lax.rem(mine + o + 1, nf)
        return pltpu.make_async_remote_copy(
            src_ref=stage.at[peer // share], dst_ref=zrecv.at[o],
            send_sem=zs_sem.at[o], recv_sem=zr_sem.at[o],
            device_id=(me, peer), device_id_type=MESH)

    steps(nf - 1, lambda o: kl_copy(o).start())
    mixed = stage[mine // share]
    for g in range(groups):
        steps(n - 1, lambda o: block_copy(g, o).wait_send())
    steps(nf - 1, lambda o: kl_copy(o).wait_send())
    steps(nf - 1, lambda o: kl_copy(o).wait_recv())
    for o in range(nf - 1):
        mixed = mixed + zrecv[o]
    result = mixed[:, :kd]
    for i in range(1, share):
        result = jnp.where(mine % share == i, mixed[:, i * kd:(i + 1) * kd], result)
    for m in range(modes):
        out[m] = result[2 * m:2 * m + 2]


def shards(visibilities, beam_modes, kl_vectors):
    n, nf = lax.axis_size("ma"), lax.axis_size("freq")
    parts, times, fcount, bases = visibilities.shape
    modes, _, _, svd, _ = beam_modes.shape
    klen, xs = kl_vectors.shape[2:]
    kd = klen // nf
    ntiles = bases // LANES
    groups, wide = ntiles // GROUP, GROUP * LANES
    rows = 2 * modes * fcount
    table_rows, table_cols = n * rows, parts * times * fcount
    table_whole = n * table_rows * table_cols <= 1 << 22
    if table_whole:
        table = jnp.asarray(np.stack([
            twiddle_rows(np, a * times, times, modes, n, fcount) for a in range(n)
        ]).astype(jnp.bfloat16))
    else:
        first = lax.axis_index("ma") * times
        table = twiddle_rows(jnp, first, times, modes, n, fcount).astype(jnp.bfloat16)
    cfg = (n, nf, modes, fcount, kd, ntiles, table_whole)
    f32, bf16 = jnp.float32, jnp.bfloat16
    dma = pltpu.SemaphoreType.DMA
    return pl.pallas_call(
        functools.partial(kernel, cfg),
        out_shape=jax.ShapeDtypeStruct((modes, 2, kd), f32),
        in_specs=[pl.BlockSpec(memory_space=pl.ANY)] * 4,
        out_specs=pl.BlockSpec(memory_space=pltpu.VMEM),
        scratch_shapes=[
            pltpu.VMEM((ntiles, parts * times, fcount, LANES), bf16),
            pltpu.VMEM((table_rows, table_cols), bf16),
            pltpu.VMEM((2, modes, fcount, svd, bases), bf16),
            pltpu.VMEM((2, modes, xs, klen), bf16),
            pltpu.VMEM((groups, n, rows, wide), f32),
            pltpu.VMEM((groups, n, rows, wide), bf16),
            pltpu.VMEM((groups, n - 1, rows, wide), bf16),
            pltpu.VMEM((klen // LANES, 2 * modes, LANES), f32),
            pltpu.VMEM((nf - 1, 2 * modes, LANES), f32),
            dma((ntiles + 5,)),
            dma((groups, n - 1)),
            dma((groups, n - 1)),
            dma((nf - 1,)),
            dma((nf - 1,)),
        ],
        compiler_params=pltpu.CompilerParams(
            collective_id=0, has_side_effects=True, vmem_limit_bytes=60 << 20),
    )(
        visibilities.reshape(parts * times, fcount, bases),
        table,
        beam_modes,
        kl_vectors.transpose(0, 1, 3, 2),
    )


def solution(mesh):
    in_specs = (
        P(None, "ma", "freq", None),
        P("ma", "freq", None, None, None),
        P("ma", None, None, "freq"),
    )
    out_specs = P("ma", None, "freq")
    return jax.shard_map(shards, mesh=mesh, in_specs=in_specs, out_specs=out_specs, check_vma=False)
```

```python
import functools
import math

import jax
import jax.numpy as jnp
import numpy as np
from jax import lax
from jax.experimental import pallas as pl
from jax.experimental.pallas import tpu as pltpu
from jax.sharding import PartitionSpec as P

NT = 4096
LANES = 128
GROUP = 4
MESH = pl.DeviceIdType.MESH


def steps(count, body):
    if count <= 16:
        for i in range(count):
            body(i)
    else:
        lax.fori_loop(0, count, lambda i, c: (body(i), c)[1], 0)


def twiddle_rows(xp, first, time_count, modes, owners, fcount):
    m = xp.arange(owners * modes, dtype=xp.int32)
    t = first + xp.arange(time_count, dtype=xp.int32)
    turns = (m[:, None] * t[None, :]) % NT
    angle = turns.astype(xp.float32) * xp.float32(2.0 * math.pi / NT)
    cos, sin = xp.cos(angle), xp.sin(angle)
    table = xp.stack([xp.stack([cos, sin], 1), xp.stack([-sin, cos], 1)], 1)
    table = table.reshape(owners, modes, 2, 2, time_count).transpose(0, 2, 1, 3, 4)
    eye = xp.eye(fcount, dtype=xp.float32)
    full = table[:, :, :, None, :, :, None] * eye[:, None, None, :]
    return full.reshape(owners * 2 * modes * fcount, 2 * time_count * fcount)


def kernel(
    cfg, vis, table, beam, kl, out,
    vbuf, tw, bbuf, kbuf, total, send, recv, stage, zrecv,
    in_sem, ssem, rsem, zs_sem, zr_sem,
):
    n, nf, modes, fcount, kd, ntiles, table_whole = cfg
    groups = ntiles // GROUP
    wide = GROUP * LANES
    rows = 2 * modes * fcount
    half = modes * fcount
    me = lax.axis_index("ma")
    mine = lax.axis_index("freq")

    tw_copy = pltpu.make_async_copy(table.at[me] if table_whole else table, tw, in_sem.at[ntiles])
    tw_copy.start()
    vis_copies = []
    for b in range(ntiles):
        copy = pltpu.make_async_copy(
            vis.at[:, :, b * LANES:(b + 1) * LANES], vbuf.at[b], in_sem.at[b])
        copy.start()
        vis_copies.append(copy)
    late = []
    for w in range(2):
        late.append(pltpu.make_async_copy(beam.at[:, :, w], bbuf.at[w], in_sem.at[ntiles + 1 + w]))
        late.append(pltpu.make_async_copy(kl.at[:, w], kbuf.at[w], in_sem.at[ntiles + 3 + w]))
    for copy in late:
        copy.start()

    barrier = pltpu.get_barrier_semaphore()

    def greet_ma(o):
        pl.semaphore_signal(barrier, inc=1, device_id=(lax.rem(me + o + 1, n), mine), device_id_type=MESH)

    def greet_freq(o):
        pl.semaphore_signal(barrier, inc=1, device_id=(me, lax.rem(mine + o + 1, nf)), device_id_type=MESH)

    steps(n - 1, greet_ma)
    steps(nf - 1, greet_freq)

    def block_copy(g, o):
        peer = lax.rem(me + o + 1, n)
        return pltpu.make_async_remote_copy(
            src_ref=send.at[g, peer], dst_ref=recv.at[g, o],
            send_sem=ssem.at[g, o], recv_sem=rsem.at[g, o],
            device_id=(peer, mine), device_id_type=MESH)

    tw_copy.wait()
    for g in range(groups):
        pieces = []
        for b in range(g * GROUP, (g + 1) * GROUP):
            vis_copies[b].wait()
            pieces.append(vbuf.at[b].reshape(vbuf.shape[1] * fcount, LANES)[...])
        part = jnp.dot(tw[...], jnp.concatenate(pieces, 1), preferred_element_type=jnp.float32)
        total[g] = part.reshape(n, rows, wide)
        send[g] = part.reshape(n, rows, wide).astype(jnp.bfloat16)
        if g == 0:
            pl.semaphore_wait(barrier, n + nf - 2)
        steps(n - 1, lambda o: block_copy(g, o).start())

    for copy in late:
        copy.wait()
    acc = jnp.zeros((rows, half * bbuf.shape[3]), jnp.float32)
    for g in range(groups):
        steps(n - 1, lambda o: block_copy(g, o).wait_recv())
        spec = total[g, me]
        if n <= 16:
            for o in range(n - 1):
                spec = spec + recv[g, o].astype(jnp.float32)
        else:
            spec = lax.fori_loop(0, n - 1, lambda o, s: s + recv[g, o].astype(jnp.float32), spec)
        turned = jnp.concatenate([-spec[half:], spec[:half]], 0)
        for w, lhs in ((0, spec), (1, turned)):
            rhs = bbuf[w, :, :, :, g * wide:(g + 1) * wide].reshape(-1, wide)
            acc = acc + lax.dot_general(
                lhs.astype(jnp.bfloat16), rhs, (((1,), (1,)), ((), ())),
                preferred_element_type=jnp.float32)

    svd = bbuf.shape[3]
    cols = half * svd
    row = lax.broadcasted_iota(jnp.int32, (half, cols), 0)
    lane = lax.broadcasted_iota(jnp.int32, (half, cols), 1)
    own = row == lane // svd
    real = jnp.sum(jnp.where(own, acc[:half], 0.0), 0, keepdims=True)
    imag = jnp.sum(jnp.where(own, acc[half:], 0.0), 0, keepdims=True)
    row = lax.broadcasted_iota(jnp.int32, (2 * modes, cols), 0)
    lane = lax.broadcasted_iota(jnp.int32, (2 * modes, cols), 1)
    own = row // 2 == lane // (fcount * svd)
    first = row % 2 == 0
    straight = jnp.where(own, jnp.where(first, real, imag), 0.0).astype(jnp.bfloat16)
    crossed = jnp.where(own, jnp.where(first, -imag, real), 0.0).astype(jnp.bfloat16)
    coeffs = jnp.dot(straight, kbuf[0].reshape(cols, -1), preferred_element_type=jnp.float32)
    coeffs = coeffs + jnp.dot(crossed, kbuf[1].reshape(cols, -1), preferred_element_type=jnp.float32)
    for i in range(stage.shape[0]):
        stage[i] = coeffs[:, i * LANES:(i + 1) * LANES]

    share = LANES // kd

    def kl_copy(o):
        peer = lax.rem(mine + o + 1, nf)
        return pltpu.make_async_remote_copy(
            src_ref=stage.at[peer // share], dst_ref=zrecv.at[o],
            send_sem=zs_sem.at[o], recv_sem=zr_sem.at[o],
            device_id=(me, peer), device_id_type=MESH)

    steps(nf - 1, lambda o: kl_copy(o).start())
    mixed = stage[mine // share]
    for g in range(groups):
        steps(n - 1, lambda o: block_copy(g, o).wait_send())
    steps(nf - 1, lambda o: kl_copy(o).wait_send())
    steps(nf - 1, lambda o: kl_copy(o).wait_recv())
    for o in range(nf - 1):
        mixed = mixed + zrecv[o]
    result = mixed[:, :kd]
    for i in range(1, share):
        result = jnp.where(mine % share == i, mixed[:, i * kd:(i + 1) * kd], result)
    for m in range(modes):
        out[m] = result[2 * m:2 * m + 2]


def shards(visibilities, beam_modes, kl_vectors):
    n, nf = lax.axis_size("ma"), lax.axis_size("freq")
    parts, times, fcount, bases = visibilities.shape
    modes, _, _, svd, _ = beam_modes.shape
    klen, xs = kl_vectors.shape[2:]
    kd = klen // nf
    ntiles = bases // LANES
    groups, wide = ntiles // GROUP, GROUP * LANES
    rows = 2 * modes * fcount
    table_rows, table_cols = n * rows, parts * times * fcount
    table_whole = n * table_rows * table_cols <= 1 << 22
    if table_whole:
        table = jnp.asarray(np.stack([
            twiddle_rows(np, a * times, times, modes, n, fcount) for a in range(n)
        ]).astype(jnp.bfloat16))
    else:
        first = lax.axis_index("ma") * times
        table = twiddle_rows(jnp, first, times, modes, n, fcount).astype(jnp.bfloat16)
    cfg = (n, nf, modes, fcount, kd, ntiles, table_whole)
    f32, bf16 = jnp.float32, jnp.bfloat16
    dma = pltpu.SemaphoreType.DMA
    return pl.pallas_call(
        functools.partial(kernel, cfg),
        out_shape=jax.ShapeDtypeStruct((modes, 2, kd), f32),
        in_specs=[pl.BlockSpec(memory_space=pl.ANY)] * 4,
        out_specs=pl.BlockSpec(memory_space=pltpu.VMEM),
        scratch_shapes=[
            pltpu.VMEM((ntiles, parts * times, fcount, LANES), bf16),
            pltpu.VMEM((table_rows, table_cols), bf16),
            pltpu.VMEM((2, modes, fcount, svd, bases), bf16),
            pltpu.VMEM((2, modes, xs, klen), bf16),
            pltpu.VMEM((groups, n, rows, wide), f32),
            pltpu.VMEM((groups, n, rows, wide), bf16),
            pltpu.VMEM((groups, n - 1, rows, wide), bf16),
            pltpu.VMEM((klen // LANES, 2 * modes, LANES), f32),
            pltpu.VMEM((nf - 1, 2 * modes, LANES), f32),
            dma((ntiles + 5,)),
            dma((groups, n - 1)),
            dma((groups, n - 1)),
            dma((nf - 1,)),
            dma((nf - 1,)),
        ],
        compiler_params=pltpu.CompilerParams(
            collective_id=0, has_side_effects=True, vmem_limit_bytes=60 << 20),
    )(
        visibilities.reshape(parts * times, fcount, bases),
        table,
        beam_modes,
        kl_vectors.transpose(0, 1, 3, 2),
    )


def solution(mesh):
    in_specs = (
        P(None, "ma", "freq", None),
        P("ma", "freq", None, None, None),
        P("ma", None, None, "freq"),
    )
    out_specs = P("ma", None, "freq")
    return jax.shard_map(shards, mesh=mesh, in_specs=in_specs, out_specs=out_specs, check_vma=False)
```
